256 devices in a mesh: freq: 64 (over y_hi, z, x), pair: 4 (over y_lo, core).
Axes of the slice: x: 4, y: 4 (y_hi: 2, y_lo: 2; y = y_hi * 2 + y_lo), z: 8, core: 2. Of those that a mesh axis runs over, the one named last changes fastest.
Arguments:
- samples: bfloat16 [2048, 64, 2, 1024], P(('freq', 'pair')), may hold values from -6 to 6
- rfi_flags: int32 [64, 1024], P('freq'), may hold values 0 or 1
- feed_map: int32 [2048], replicated, may hold values from 0 to 2047, each once
Outputs:
- visibilities: bfloat16 [64, 2, 2048, 2048], P('freq', None, 'pair')
The draws below stay inside these ranges and needn't reach their ends.
Inputs may be any that keep to these rules, and one draw needn't show every extreme that they name: `feed_map`: each of the 2048 feeds is assigned to exactly one slot.
All inputs are finite; a program needn't handle non-finite values. No bound on the sum of `rfi_flags` on one device may be relied on, other than what follows from the above.
Results may differ from the reference program's by a relative error of at most 0.001.
Values may be sent and summed in bfloat16 or wider, within the bound.
A program may use at most 64 MiB of HBM per device.

```python
import jax
import jax.numpy as jnp
from jax import lax

F = 2048
TS = 1024
CH = 64


def touch_ends(array, stream_key, smallest, largest):
    dims = array.shape
    spot = [jax.random.randint(jax.random.fold_in(stream_key, axis), (), 0, dims[axis]) for axis in range(len(dims))]
    array = array.at[tuple(spot)].set(smallest)
    longest = dims.index(max(dims))
    spot[longest] = (spot[longest] + 1) % dims[longest]
    return array.at[tuple(spot)].set(largest)


def steps_of(own_key, shape, pieces, low, top_value):
    level = 1.0
    for dim, shards_of in pieces:
        steps = jax.random.uniform(jax.random.fold_in(jax.random.fold_in(own_key, 6), dim), (shards_of,), jnp.float32, low / len(pieces), top_value / len(pieces))
        level = level * jnp.repeat(jnp.exp(steps), shape[dim] // shards_of).reshape((-1,) + (1,) * (len(shape) - 1 - dim))
    return level


def gaussian(own_key, extent, scale, reach, split=(), kind=jnp.bfloat16):
    values = scale * jax.random.normal(own_key, extent, jnp.float32)
    if split:
        values = values * steps_of(own_key, extent, split, -0.22, 0.18)
    return jnp.clip(values, -reach, reach).astype(kind)


def setup_inputs(seed: int = 0) -> dict:
    arg_keys = jax.random.split(jax.random.key(seed), 4)
    samples = gaussian(arg_keys[0], (F, CH, 2, TS), 1.0, 6.0, ((0, 256),))
    rfi_flags = touch_ends((jax.random.randint(arg_keys[1], (CH, TS), 0, 4) < 1).astype(jnp.int32), jax.random.fold_in(arg_keys[1], 1), 0, 1)
    feed_map = jax.random.permutation(arg_keys[2], F).astype(jnp.int32)
    return {"samples": samples, "rfi_flags": rfi_flags, "feed_map": feed_map}


def reference(samples, rfi_flags, feed_map):
    keep_mask = (1 - rfi_flags).astype(jnp.bfloat16)

    def channel_vis(channel):
        samples_one = lax.dynamic_index_in_dim(samples, channel, 1, keepdims=False)
        keep_row = lax.dynamic_index_in_dim(keep_mask, channel, 0, keepdims=False)
        flagged = (samples_one * keep_row[None, None, :]).astype(jnp.bfloat16)
        ordered = jnp.take(flagged, feed_map, axis=0)
        parts = ordered.reshape(F, 2 * TS)
        swapped = jnp.concatenate([ordered[:, 1, :], -ordered[:, 0, :]], axis=1)
        stacked = jnp.concatenate([parts, swapped], axis=0)
        product = jnp.dot(stacked, parts.T, preferred_element_type=jnp.float32) * (1.0 / TS)
        return product.reshape(2, F, F).astype(jnp.bfloat16)

    return lax.map(channel_vis, jnp.arange(CH, dtype=jnp.int32))
```

```python
import jax
import jax.numpy as jnp
from jax import lax
from jax.experimental import pallas as pl
from jax.experimental.pallas import tpu as pltpu
from jax.sharding import PartitionSpec as P

MESH = pl.DeviceIdType.MESH
NC = 8
TC = 128
SLOTS = 2048
ROWS = 512


def kernel(samples, mask, slot_rows, out, zbuf, obuf, g, onehot, merged, ordered, left, acc, staged,
           zs, zr, xs, xr, own_s, own_r, out_s, out_r, fwd_s, fwd_r, core_s, core_r, write_s):
    fi = lax.axis_index("freq")
    member = lax.axis_index("pair")
    yh, z, x = fi // 32, (fi // 4) % 8, fi % 4
    yl, core = member // 2, member % 2
    y = yh * 2 + yl
    y_inner = yh * 2 + 1 - yl
    y_outer = 3 - y
    y_far = (1 - yh) * 2 + yl
    zpeers = [lax.rem(z + d, 8) for d in (4, 3, 5, 2, 6, 1, 7)]
    xpeers = [lax.rem(x + d, 4) for d in (2, 1, 3)]

    def device(yy, zz, xx, cc):
        return ((yy // 2 * 8 + zz) * 4 + xx, yy % 2 * 2 + cc)

    inner = device(y_inner, z, x, core)
    outer = device(y_outer, z, x, core)
    sibling = device(y, z, x, 1 - core)

    def remote(src, dst, send, recv, target):
        return pltpu.make_async_remote_copy(
            src_ref=src, dst_ref=dst, send_sem=send, recv_sem=recv, device_id=target, device_id_type=MESH
        )

    def wait(ref, sem):
        pltpu.make_async_copy(ref, ref, sem).wait()

    barrier = pltpu.get_barrier_semaphore()
    targets = [device(y, zz, x, core) for zz in zpeers] + [device(y, z, xx, core) for xx in xpeers]
    targets += [inner, outer, sibling]
    for target in targets:
        pl.semaphore_signal(barrier, inc=1, device_id=target, device_id_type=MESH)
    pl.semaphore_wait(barrier, len(targets))

    def z_send(j):
        k, h = j // 2, j % 2
        half = jnp.where(h == 0, 1 - yh, yh)
        pltpu.make_async_copy(samples.at[k, half, z], zbuf.at[j, z], zr.at[j]).start()
        for zz in zpeers:
            remote(samples.at[k, half, zz], zbuf.at[j, z], zs.at[j], zr.at[j], device(y, zz, x, core)).start()

    def x_send(k, h):
        j = 2 * k + h
        wait(zbuf.at[j], zr.at[j])
        dst = g.at[k, core, y, x] if h else obuf.at[k, x]
        pltpu.make_async_copy(zbuf.at[j, :, x], dst, xr.at[j]).start()
        for xx in xpeers:
            remote(zbuf.at[j, :, xx], dst, xs.at[j], xr.at[j], device(y, z, xx, core)).start()

    def core_send(k, yy):
        remote(g.at[k, core, yy], g.at[k, core, yy], core_s.at[k], core_r.at[k], sibling).start()

    def y_send(k, h):
        j = 2 * k + h
        if h:
            wait(g.at[k, core, y], xr.at[j])
            remote(g.at[k, core, y], g.at[k, core, y], own_s.at[k], own_r.at[k], inner).start()
            core_send(k, y)
        else:
            wait(obuf.at[k], xr.at[j])
            remote(obuf.at[k], g.at[k, core, y], out_s.at[k], out_r.at[k], outer).start()

    def forward(k):
        block = g.at[k, core, y_outer]
        wait(block, out_r.at[k])
        remote(block, block, fwd_s.at[k], fwd_r.at[k], inner).start()
        core_send(k, y_outer)

    def own_arrived(k):
        wait(g.at[k, core, y_inner], own_r.at[k])
        core_send(k, y_inner)

    def forward_arrived(k):
        wait(g.at[k, core, y_far], fwd_r.at[k])
        core_send(k, y_far)

    def permute(k, block):
        @pl.loop(0, 2)
        def _(i):
            rows = pl.ds(pl.multiple_of(block * 1024 + i * 512, 512), 512)
            ordered[rows, :] = jnp.dot(
                onehot[rows, :], merged[...], preferred_element_type=jnp.float32
            ).astype(jnp.bfloat16)

    def start_compute(k):
        wait(g.at[k, 1 - core], core_r.at[k])
        keep = mask[k]

        @pl.loop(0, 8)
        def _(b):
            rows = pl.ds(pl.multiple_of(b * 256, 256), 256)
            block = g[k, b // 4, b % 4].reshape(32, 16, TC) * keep
            merged[rows, :TC] = block[:, :8].reshape(256, TC)
            merged[rows, TC:] = block[:, 8:].reshape(256, TC)

        permute(k, 0)

    def prepare_left():
        own = ordered[pl.ds(pl.multiple_of(member * ROWS, ROWS), ROWS), :]
        left[:ROWS, :] = own
        left[ROWS:, :TC] = own[:, TC:]
        left[ROWS:, TC:] = -own[:, :TC]

    def product(k, half):
        @pl.when(k < NC - 1)
        def _():
            @pl.loop(0, 2)
            def _(i):
                n = half * 2 + i
                rows = pl.ds(pl.multiple_of(n * 512, 512), 512)
                acc[n] += lax.dot_general(
                    left[...], ordered[rows, :], (((1,), (1,)), ((), ())), preferred_element_type=jnp.float32
                )

        @pl.when(k == NC - 1)
        def _():
            @pl.loop(0, 2)
            def _(i):
                n = half * 2 + i
                rows = pl.ds(pl.multiple_of(n * 512, 512), 512)
                total = acc[n] + lax.dot_general(
                    left[...], ordered[rows, :], (((1,), (1,)), ((), ())), preferred_element_type=jnp.float32
                )
                staged[n] = (total * (1.0 / (NC * TC))).astype(jnp.bfloat16).reshape(2, ROWS, 512)
                pltpu.make_async_copy(staged.at[n], out.at[0, :, :, rows], write_s.at[n]).start()

    for j in range(4):
        z_send(j)

    @pl.loop(0, 16)
    def _(b):
        rows = pl.ds(pl.multiple_of(b * 128, 128), 128)
        spot = slot_rows[rows, :]
        hit = spot == lax.broadcasted_iota(jnp.int32, (128, SLOTS), 1)
        onehot[rows, :] = jnp.where(hit, 1.0, 0.0).astype(jnp.bfloat16)

    @pl.loop(0, 4)
    def _(n):
        acc[n] = jnp.zeros((2 * ROWS, 512), jnp.float32)

    def step(s, carry):
        @pl.when(s < NC)
        def _():
            x_send(s, 0)

        @pl.when(s + 2 < NC)
        def _():
            z_send(2 * s + 4)

        @pl.when(s >= 2)
        def _():
            start_compute(s - 2)

        @pl.when((s >= 1) & (s < NC + 1))
        def _():
            own_arrived(s - 1)

        @pl.when(s < NC)
        def _():
            y_send(s, 0)

        @pl.when(s >= 2)
        def _():
            permute(s - 2, 1)

        @pl.when(s < NC)
        def _():
            x_send(s, 1)

        @pl.when(s + 2 < NC)
        def _():
            z_send(2 * s + 5)

        @pl.when(s >= 2)
        def _():
            prepare_left()
            product(s - 2, 0)

        @pl.when(s < NC)
        def _():
            y_send(s, 1)
            forward(s)

        @pl.when((s >= 1) & (s < NC + 1))
        def _():
            forward_arrived(s - 1)

        @pl.when(s >= 2)
        def _():
            product(s - 2, 1)

        return carry

    lax.fori_loop(0, NC + 2, step, 0)

    @pl.loop(0, NC)
    def _(k):
        for h in range(2):
            wait(zbuf.at[2 * k + h, pl.ds(0, 7)], zs.at[2 * k + h])
            wait(obuf.at[k, pl.ds(0, 3)], xs.at[2 * k + h])
        wait(obuf.at[k], own_s.at[k])
        wait(obuf.at[k], out_s.at[k])
        wait(obuf.at[k], fwd_s.at[k])
        wait(g.at[k, 0], core_s.at[k])

    @pl.loop(0, 4)
    def _(n):
        rows = pl.ds(pl.multiple_of(n * 512, 512), 512)
        pltpu.make_async_copy(staged.at[n], out.at[0, :, :, rows], write_s.at[n]).wait()


def local(samples, rfi_flags, feed_map):
    feeds = samples.shape[0]
    turned = samples.reshape(feeds, 2, 8, 4, 2, NC, TC).transpose(5, 1, 2, 3, 4, 0, 6)
    turned = turned.reshape(NC, 2, 8, 4, 2 * feeds, TC)
    mask = (1 - rfi_flags).astype(jnp.bfloat16).reshape(NC, 1, TC)
    mask = jnp.broadcast_to(mask, (NC, 2 * feeds, TC))
    w, shard = feed_map % 8, feed_map // 8
    core, yl, x, z, yh = shard % 2, shard // 2 % 2, shard // 4 % 4, shard // 16 % 8, shard // 128
    spot = (((core * 4 + yh * 2 + yl) * 4 + x) * 8 + z) * 8 + w
    dma = pltpu.SemaphoreType.DMA
    vmem = pl.BlockSpec(memory_space=pltpu.VMEM)
    return pl.pallas_call(
        kernel,
        out_shape=jax.ShapeDtypeStruct((1, 2, ROWS, SLOTS), jnp.bfloat16),
        in_specs=[pl.BlockSpec(memory_space=pl.ANY), vmem, vmem],
        out_specs=pl.BlockSpec(memory_space=pl.ANY),
        scratch_shapes=[
            pltpu.VMEM((2 * NC, 8, 4, 16, TC), jnp.bfloat16),
            pltpu.VMEM((NC, 4, 8, 16, TC), jnp.bfloat16),
            pltpu.VMEM((NC, 2, 4, 4, 8, 16, TC), jnp.bfloat16),
            pltpu.VMEM((SLOTS, SLOTS), jnp.bfloat16),
            pltpu.VMEM((SLOTS, 2 * TC), jnp.bfloat16),
            pltpu.VMEM((SLOTS, 2 * TC), jnp.bfloat16),
            pltpu.VMEM((2 * ROWS, 2 * TC), jnp.bfloat16),
            pltpu.VMEM((4, 2 * ROWS, 512), jnp.float32),
            pltpu.VMEM((4, 2, ROWS, 512), jnp.bfloat16),
            dma((2 * NC,)), dma((2 * NC,)), dma((2 * NC,)), dma((2 * NC,)),
            dma((NC,)), dma((NC,)), dma((NC,)), dma((NC,)), dma((NC,)), dma((NC,)), dma((NC,)), dma((NC,)),
            dma((4,)),
        ],
        compiler_params=pltpu.CompilerParams(
            collective_id=0, has_side_effects=True, vmem_limit_bytes=56 * 1024 * 1024
        ),
        cost_estimate=pl.CostEstimate(flops=26 * 10**9, bytes_accessed=6 * 2**20, transcendentals=0),
        name="correlate",
    )(turned, mask, spot.reshape(SLOTS, 1))


def solution(mesh):
    in_specs = (P(("freq", "pair"), None, None, None), P("freq", None), P())
    out_specs = P("freq", None, "pair", None)
    return jax.shard_map(local, mesh=mesh, in_specs=in_specs, out_specs=out_specs, check_vma=False)
```

```python
import jax
import jax.numpy as jnp
from jax import lax
from jax.experimental import pallas as pl
from jax.experimental.pallas import tpu as pltpu
from jax.sharding import PartitionSpec as P

MESH = pl.DeviceIdType.MESH
NC = 8
TC = 128
SLOTS = 2048
ROWS = 512


def kernel(raw_samples, flags, feeds, out, raw, samples, zbuf, obuf, g, onehot, merged, ordered, left, acc, staged,
           zs, zr, xs, xr, own_s, own_r, out_s, out_r, fwd_s, fwd_r, core_s, core_r, pair_s, pair_r, write_s, raw_s):
    fi = lax.axis_index("freq")
    member = lax.axis_index("pair")
    yh, z, x = fi // 32, (fi // 4) % 8, fi % 4
    yl, core = member // 2, member % 2
    y = yh * 2 + yl
    y_inner = yh * 2 + 1 - yl
    y_outer = 3 - y
    y_far = (1 - yh) * 2 + yl
    zpeers = [lax.rem(z + d, 8) for d in (4, 3, 5, 2, 6, 1, 7)]
    xpeers = [lax.rem(x + d, 4) for d in (2, 1, 3)]

    def device(yy, zz, xx, cc):
        return ((yy // 2 * 8 + zz) * 4 + xx, yy % 2 * 2 + cc)

    inner = device(y_inner, z, x, core)
    outer = device(y_outer, z, x, core)
    sibling = device(y, z, x, 1 - core)

    def remote(src, dst, send, recv, target):
        return pltpu.make_async_remote_copy(
            src_ref=src, dst_ref=dst, send_sem=send, recv_sem=recv, device_id=target, device_id_type=MESH
        )

    def wait(ref, sem):
        pltpu.make_async_copy(ref, ref, sem).wait()

    load = pltpu.make_async_copy(raw_samples, raw, raw_s)
    load.start()
    barrier = pltpu.get_barrier_semaphore()
    targets = [device(y, zz, x, core) for zz in zpeers] + [device(y, z, xx, core) for xx in xpeers]
    targets += [inner, outer, sibling]
    for target in targets:
        pl.semaphore_signal(barrier, inc=1, device_id=target, device_id_type=MESH)

    def pack(k):
        times = pl.ds(pl.multiple_of(k * TC, TC), TC)

        @pl.loop(0, 8)
        def _(b):
            block = raw[:, pl.ds(pl.multiple_of(b * 8, 8), 8), :, times]
            packed = jnp.transpose(block, (1, 2, 0, 3)).reshape(2, 4, 16, TC)
            samples[k, b // 4, pl.ds(pl.multiple_of(b % 4 * 2, 2), 2)] = packed


    def z_send(j):
        k, h = j // 2, j % 2
        half = jnp.where(h == 0, 1 - yh, yh)
        pltpu.make_async_copy(samples.at[k, half, z], zbuf.at[j, z], zr.at[j]).start()
        for zz in zpeers:
            remote(samples.at[k, half, zz], zbuf.at[j, z], zs.at[j], zr.at[j], device(y, zz, x, core)).start()

    def x_send(k, h):
        j = 2 * k + h
        wait(zbuf.at[j], zr.at[j])
        dst = g.at[k, core, y, x] if h else obuf.at[k, x]
        pltpu.make_async_copy(zbuf.at[j, :, x], dst, xr.at[j]).start()
        for xx in xpeers:
            remote(zbuf.at[j, :, xx], dst, xs.at[j], xr.at[j], device(y, z, xx, core)).start()

    def core_send(k, yy):
        remote(g.at[k, core, yy], g.at[k, core, yy], core_s.at[k], core_r.at[k], sibling).start()

    def y_send(k, h):
        j = 2 * k + h
        if h:
            wait(g.at[k, core, y], xr.at[j])
            remote(g.at[k, core, y], g.at[k, core, y], own_s.at[k], own_r.at[k], inner).start()
            core_send(k, y)
        else:
            wait(obuf.at[k], xr.at[j])
            remote(obuf.at[k], g.at[k, core, y], out_s.at[k], out_r.at[k], outer).start()

    def forward(k):
        block = g.at[k, core, y_outer]
        wait(block, out_r.at[k])
        remote(block, block, fwd_s.at[k], fwd_r.at[k], inner).start()
        core_send(k, y_outer)

    def own_arrived(k):
        wait(g.at[k, core, y_inner], own_r.at[k])
        core_send(k, y_inner)

    def forward_arrived(k):
        wait(g.at[k, core, y_far], fwd_r.at[k])
        core_send(k, y_far)

    def order(k):
        wait(g.at[k, 1 - core], core_r.at[k])
        times = pl.ds(pl.multiple_of(k * TC, TC), TC)
        keep = jnp.broadcast_to((1 - flags[:, times]).astype(jnp.float32), (16, TC)).astype(jnp.bfloat16)

        @pl.loop(0, 8)
        def _(b):
            rows = pl.ds(pl.multiple_of(b * 256, 256), 256)
            block = g[k, b // 4, b % 4].reshape(32, 16, TC) * keep
            merged[rows, :TC] = block[:, :8].reshape(256, TC)
            merged[rows, TC:] = block[:, 8:].reshape(256, TC)

        picked = jnp.dot(onehot[...], merged[...], preferred_element_type=jnp.float32).astype(jnp.bfloat16)
        ordered[k, :, core] = picked.reshape(2, ROWS, 2 * TC)
        pair_copy(k).start()

    def pair_copy(k):
        block = ordered.at[k, :, core]
        return remote(block, block, pair_s.at[k], pair_r.at[k], sibling)

    def prepare_left(k):
        own = ordered[k, yl, core]
        left[:ROWS, :] = own
        left[ROWS:, :TC] = own[:, TC:]
        left[ROWS:, TC:] = -own[:, :TC]

    def multiply(k, half):
        return lax.dot_general(
            left[...],
            ordered[k, :, half].reshape(2 * ROWS, 2 * TC),
            (((1,), (1,)), ((), ())),
            preferred_element_type=jnp.float32,
        )

    def write(half, i):
        columns = pl.ds(pl.multiple_of((i * 2 + half) * ROWS, ROWS), ROWS)
        return pltpu.make_async_copy(staged.at[half, i], out.at[0, :, :, columns], write_s.at[half, i])

    def product(k, half):
        @pl.when(k < NC - 1)
        def _():
            acc[half] += multiply(k, half)

        @pl.when(k == NC - 1)
        def _():
            total = (acc[half] + multiply(k, half)) * (1.0 / (NC * TC))
            for i in range(2):
                staged[half, i] = total[:, i * ROWS : (i + 1) * ROWS].astype(jnp.bfloat16).reshape(2, ROWS, ROWS)
                write(half, i).start()

    load.wait()
    pack(0)
    pl.semaphore_wait(barrier, len(targets))
    z_send(0)
    z_send(1)
    pack(1)
    z_send(2)
    z_send(3)

    @pl.loop(0, 8)
    def _(b):
        feed = feeds[pl.ds((b // 4 * 2 + core) * 4 + b % 4, 1), :]
        w, c, l = feed & 7, (feed >> 3) & 1, (feed >> 4) & 1
        xx, zz, h = (feed >> 5) & 3, (feed >> 7) & 7, feed >> 10
        spot = ((((c * 4 + h * 2 + l) * 4 + xx) * 8 + zz) * 8 + w).astype(jnp.float32)
        spot = jnp.broadcast_to(spot, (128, 128)).T.astype(jnp.int32)
        for n in range(SLOTS // 128):
            hit = spot == lax.broadcasted_iota(jnp.int32, (128, 128), 1) + n * 128
            onehot[pl.ds(pl.multiple_of(b * 128, 128), 128), n * 128 : (n + 1) * 128] = jnp.where(
                hit, 1.0, 0.0
            ).astype(jnp.bfloat16)

    for half in range(2):
        acc[half] = jnp.zeros((2 * ROWS, 2 * ROWS), jnp.float32)

    def step(s, carry):
        @pl.when(s < NC)
        def _():
            x_send(s, 0)

        @pl.when(s + 2 < NC)
        def _():
            pack(s + 2)
            z_send(2 * s + 4)

        @pl.when((s >= 1) & (s < NC + 1))
        def _():
            y_send((s - 1), 0)

        @pl.when((s >= 1) & (s < NC + 1))
        def _():
            y_send((s - 1), 1)

        @pl.when((s >= 2) & (s < NC + 2))
        def _():
            forward((s - 2))

        @pl.when(s >= 4)
        def _():
            order((s - 4))

        @pl.when(s < NC)
        def _():
            x_send(s, 1)

        @pl.when(s + 2 < NC)
        def _():
            z_send(2 * s + 5)

        @pl.when(s >= 4)
        def _():
            prepare_left((s - 4))
            product((s - 4), core)

        @pl.when((s >= 2) & (s < NC + 2))
        def _():
            own_arrived((s - 2))

        @pl.when(s >= 4)
        def _():
            wait(ordered.at[(s - 4), :, 1 - core], pair_r.at[(s - 4)])
            product((s - 4), 1 - core)

        @pl.when((s >= 3) & (s < NC + 3))
        def _():
            forward_arrived((s - 3))

        return carry

    lax.fori_loop(0, NC + 4, step, 0)

    @pl.loop(0, NC)
    def _(k):
        for h in range(2):
            wait(zbuf.at[2 * k + h, pl.ds(0, 7)], zs.at[2 * k + h])
            wait(obuf.at[k, pl.ds(0, 3)], xs.at[2 * k + h])
        wait(obuf.at[k], own_s.at[k])
        wait(obuf.at[k], out_s.at[k])
        wait(obuf.at[k], fwd_s.at[k])
        wait(g.at[k, 0], core_s.at[k])
        wait(ordered.at[k, :, core], pair_s.at[k])

    for half in range(2):
        for i in range(2):
            write(half, i).wait()


def local(samples, rfi_flags, feed_map):
    dma = pltpu.SemaphoreType.DMA
    vmem = pl.BlockSpec(memory_space=pltpu.VMEM)
    return pl.pallas_call(
        kernel,
        out_shape=jax.ShapeDtypeStruct((1, 2, ROWS, SLOTS), jnp.bfloat16),
        in_specs=[pl.BlockSpec(memory_space=pltpu.HBM), vmem, vmem],
        out_specs=pl.BlockSpec(memory_space=pl.ANY),
        scratch_shapes=[
            pltpu.VMEM((8, 64, 2, NC * TC), jnp.bfloat16),
            pltpu.VMEM((NC, 2, 8, 4, 16, TC), jnp.bfloat16),
            pltpu.VMEM((2 * NC, 8, 4, 16, TC), jnp.bfloat16),
            pltpu.VMEM((NC, 4, 8, 16, TC), jnp.bfloat16),
            pltpu.VMEM((NC, 2, 4, 4, 8, 16, TC), jnp.bfloat16),
            pltpu.VMEM((2 * ROWS, SLOTS), jnp.bfloat16),
            pltpu.VMEM((SLOTS, 2 * TC), jnp.bfloat16),
            pltpu.VMEM((NC, 2, 2, ROWS, 2 * TC), jnp.bfloat16),
            pltpu.VMEM((2 * ROWS, 2 * TC), jnp.bfloat16),
            pltpu.VMEM((2, 2 * ROWS, 2 * ROWS), jnp.float32),
            pltpu.VMEM((2, 2, 2, ROWS, ROWS), jnp.bfloat16),
            dma((2 * NC,)), dma((2 * NC,)), dma((2 * NC,)), dma((2 * NC,)),
            dma((NC,)), dma((NC,)), dma((NC,)), dma((NC,)), dma((NC,)), dma((NC,)), dma((NC,)), dma((NC,)),
            dma((NC,)), dma((NC,)), dma((2, 2)), dma,
        ],
        compiler_params=pltpu.CompilerParams(
            collective_id=0, has_side_effects=True, vmem_limit_bytes=46 * 1024 * 1024
        ),
        cost_estimate=pl.CostEstimate(flops=26 * 10**9, bytes_accessed=6 * 2**20, transcendentals=0),
        name="correlate",
    )(samples, rfi_flags, feed_map.reshape(16, 128))


def solution(mesh):
    in_specs = (P(("freq", "pair"), None, None, None), P("freq", None), P())
    out_specs = P("freq", None, "pair", None)
    return jax.shard_map(local, mesh=mesh, in_specs=in_specs, out_specs=out_specs, check_vma=False)
```

```python
import jax
import jax.numpy as jnp
from jax import lax
from jax.experimental import pallas as pl
from jax.experimental.pallas import tpu as pltpu
from jax.sharding import PartitionSpec as P

MESH = pl.DeviceIdType.MESH
NC = 8
TC = 128
SLOTS = 2048
ROWS = 512


def kernel(raw, flags, feeds, out, samples, zbuf, obuf, g, onehot, merged, ordered, left, acc, staged,
           zs, zr, xs, xr, own_s, own_r, out_s, out_r, fwd_s, fwd_r, core_s, core_r, pair_s, pair_r, write_s):
    fi = lax.axis_index("freq")
    member = lax.axis_index("pair")
    yh, z, x = fi // 32, (fi // 4) % 8, fi % 4
    yl, core = member // 2, member % 2
    y = yh * 2 + yl
    y_inner = yh * 2 + 1 - yl
    y_outer = 3 - y
    y_far = (1 - yh) * 2 + yl
    zpeers = [lax.rem(z + d, 8) for d in (4, 3, 5, 2, 6, 1, 7)]
    xpeers = [lax.rem(x + d, 4) for d in (2, 1, 3)]

    def device(yy, zz, xx, cc):
        return ((yy // 2 * 8 + zz) * 4 + xx, yy % 2 * 2 + cc)

    inner = device(y_inner, z, x, core)
    outer = device(y_outer, z, x, core)
    sibling = device(y, z, x, 1 - core)

    def remote(src, dst, send, recv, target):
        return pltpu.make_async_remote_copy(
            src_ref=src, dst_ref=dst, send_sem=send, recv_sem=recv, device_id=target, device_id_type=MESH
        )

    def wait(ref, sem):
        pltpu.make_async_copy(ref, ref, sem).wait()

    barrier = pltpu.get_barrier_semaphore()
    targets = [device(y, zz, x, core) for zz in zpeers] + [device(y, z, xx, core) for xx in xpeers]
    targets += [inner, outer, sibling]
    for target in targets:
        pl.semaphore_signal(barrier, inc=1, device_id=target, device_id_type=MESH)

    def pack(k):
        times = pl.ds(pl.multiple_of(k * TC, TC), TC)

        @pl.loop(0, 8)
        def _(b):
            block = raw[:, pl.ds(pl.multiple_of(b * 8, 8), 8), :, times]
            packed = jnp.transpose(block, (1, 2, 0, 3)).reshape(2, 4, 16, TC)
            samples[k, b // 4, pl.ds(pl.multiple_of(b % 4 * 2, 2), 2)] = packed


    def z_send(j):
        k, h = j // 2, j % 2
        half = jnp.where(h == 0, 1 - yh, yh)
        pltpu.make_async_copy(samples.at[k, half, z], zbuf.at[j, z], zr.at[j]).start()
        for zz in zpeers:
            remote(samples.at[k, half, zz], zbuf.at[j, z], zs.at[j], zr.at[j], device(y, zz, x, core)).start()

    def x_send(k, h):
        j = 2 * k + h
        wait(zbuf.at[j], zr.at[j])
        dst = g.at[k, core, y, x] if h else obuf.at[k, x]
        pltpu.make_async_copy(zbuf.at[j, :, x], dst, xr.at[j]).start()
        for xx in xpeers:
            remote(zbuf.at[j, :, xx], dst, xs.at[j], xr.at[j], device(y, z, xx, core)).start()

    def core_send(k, yy):
        remote(g.at[k, core, yy], g.at[k, core, yy], core_s.at[k], core_r.at[k], sibling).start()

    def y_send(k, h):
        j = 2 * k + h
        if h:
            wait(g.at[k, core, y], xr.at[j])
            remote(g.at[k, core, y], g.at[k, core, y], own_s.at[k], own_r.at[k], inner).start()
            core_send(k, y)
        else:
            wait(obuf.at[k], xr.at[j])
            remote(obuf.at[k], g.at[k, core, y], out_s.at[k], out_r.at[k], outer).start()

    def forward(k):
        block = g.at[k, core, y_outer]
        wait(block, out_r.at[k])
        remote(block, block, fwd_s.at[k], fwd_r.at[k], inner).start()
        core_send(k, y_outer)

    def own_arrived(k):
        wait(g.at[k, core, y_inner], own_r.at[k])
        core_send(k, y_inner)

    def forward_arrived(k):
        wait(g.at[k, core, y_far], fwd_r.at[k])
        core_send(k, y_far)

    def order(k):
        wait(g.at[k, 1 - core], core_r.at[k])
        times = pl.ds(pl.multiple_of(k * TC, TC), TC)
        keep = jnp.broadcast_to((1 - flags[:, times]).astype(jnp.float32), (16, TC)).astype(jnp.bfloat16)

        @pl.loop(0, 8)
        def _(b):
            rows = pl.ds(pl.multiple_of(b * 256, 256), 256)
            block = g[k, b // 4, b % 4].reshape(32, 16, TC) * keep
            merged[rows, :TC] = block[:, :8].reshape(256, TC)
            merged[rows, TC:] = block[:, 8:].reshape(256, TC)

        picked = jnp.dot(onehot[...], merged[...], preferred_element_type=jnp.float32).astype(jnp.bfloat16)
        ordered[k, :, core] = picked.reshape(2, ROWS, 2 * TC)
        pair_copy(k).start()

    def pair_copy(k):
        block = ordered.at[k, :, core]
        return remote(block, block, pair_s.at[k], pair_r.at[k], sibling)

    def prepare_left(k):
        own = ordered[k, yl, core]
        left[:ROWS, :] = own
        left[ROWS:, :TC] = own[:, TC:]
        left[ROWS:, TC:] = -own[:, :TC]

    def multiply(k, half):
        return lax.dot_general(
            left[...],
            ordered[k, :, half].reshape(2 * ROWS, 2 * TC),
            (((1,), (1,)), ((), ())),
            preferred_element_type=jnp.float32,
        )

    def write(half, i):
        columns = pl.ds(pl.multiple_of((i * 2 + half) * ROWS, ROWS), ROWS)
        return pltpu.make_async_copy(staged.at[half, i], out.at[0, :, :, columns], write_s.at[half, i])

    def product(k, half):
        @pl.when(k < NC - 1)
        def _():
            acc[half] += multiply(k, half)

        @pl.when(k == NC - 1)
        def _():
            total = (acc[half] + multiply(k, half)) * (1.0 / (NC * TC))
            for i in range(2):
                staged[half, i] = total[:, i * ROWS : (i + 1) * ROWS].astype(jnp.bfloat16).reshape(2, ROWS, ROWS)
                write(half, i).start()

    pack(0)
    pl.semaphore_wait(barrier, len(targets))
    z_send(0)
    z_send(1)
    pack(1)
    z_send(2)
    z_send(3)

    @pl.loop(0, 8)
    def _(b):
        feed = feeds[pl.ds((b // 4 * 2 + core) * 4 + b % 4, 1), :]
        w, c, l = feed & 7, (feed >> 3) & 1, (feed >> 4) & 1
        xx, zz, h = (feed >> 5) & 3, (feed >> 7) & 7, feed >> 10
        spot = ((((c * 4 + h * 2 + l) * 4 + xx) * 8 + zz) * 8 + w).astype(jnp.float32)
        spot = jnp.broadcast_to(spot, (128, 128)).T.astype(jnp.int32)
        for n in range(SLOTS // 128):
            hit = spot == lax.broadcasted_iota(jnp.int32, (128, 128), 1) + n * 128
            onehot[pl.ds(pl.multiple_of(b * 128, 128), 128), n * 128 : (n + 1) * 128] = jnp.where(
                hit, 1.0, 0.0
            ).astype(jnp.bfloat16)

    for half in range(2):
        acc[half] = jnp.zeros((2 * ROWS, 2 * ROWS), jnp.float32)

    def step(s, carry):
        @pl.when(s < NC)
        def _():
            x_send(s, 0)

        @pl.when(s + 2 < NC)
        def _():
            pack(s + 2)
            z_send(2 * s + 4)

        @pl.when((s >= 1) & (s < NC + 1))
        def _():
            y_send((s - 1), 0)

        @pl.when(s < NC)
        def _():
            x_send(s, 1)

        @pl.when(s + 2 < NC)
        def _():
            z_send(2 * s + 5)

        @pl.when((s >= 1) & (s < NC + 1))
        def _():
            y_send((s - 1), 1)

        @pl.when(s >= 4)
        def _():
            order((s - 4))

        @pl.when((s >= 2) & (s < NC + 2))
        def _():
            forward((s - 2))

        @pl.when(s >= 4)
        def _():
            prepare_left((s - 4))
            product((s - 4), core)

        @pl.when((s >= 2) & (s < NC + 2))
        def _():
            own_arrived((s - 2))

        @pl.when(s >= 4)
        def _():
            wait(ordered.at[(s - 4), :, 1 - core], pair_r.at[(s - 4)])
            product((s - 4), 1 - core)

        @pl.when((s >= 3) & (s < NC + 3))
        def _():
            forward_arrived((s - 3))

        return carry

    lax.fori_loop(0, NC + 4, step, 0)

    @pl.loop(0, NC)
    def _(k):
        for h in range(2):
            wait(zbuf.at[2 * k + h, pl.ds(0, 7)], zs.at[2 * k + h])
            wait(obuf.at[k, pl.ds(0, 3)], xs.at[2 * k + h])
        wait(obuf.at[k], own_s.at[k])
        wait(obuf.at[k], out_s.at[k])
        wait(obuf.at[k], fwd_s.at[k])
        wait(g.at[k, 0], core_s.at[k])
        wait(ordered.at[k, :, core], pair_s.at[k])

    for half in range(2):
        for i in range(2):
            write(half, i).wait()


def local(samples, rfi_flags, feed_map):
    dma = pltpu.SemaphoreType.DMA
    vmem = pl.BlockSpec(memory_space=pltpu.VMEM)
    return pl.pallas_call(
        kernel,
        out_shape=jax.ShapeDtypeStruct((1, 2, ROWS, SLOTS), jnp.bfloat16),
        in_specs=[vmem, vmem, vmem],
        out_specs=pl.BlockSpec(memory_space=pl.ANY),
        scratch_shapes=[
            pltpu.VMEM((NC, 2, 8, 4, 16, TC), jnp.bfloat16),
            pltpu.VMEM((2 * NC, 8, 4, 16, TC), jnp.bfloat16),
            pltpu.VMEM((NC, 4, 8, 16, TC), jnp.bfloat16),
            pltpu.VMEM((NC, 2, 4, 4, 8, 16, TC), jnp.bfloat16),
            pltpu.VMEM((2 * ROWS, SLOTS), jnp.bfloat16),
            pltpu.VMEM((SLOTS, 2 * TC), jnp.bfloat16),
            pltpu.VMEM((NC, 2, 2, ROWS, 2 * TC), jnp.bfloat16),
            pltpu.VMEM((2 * ROWS, 2 * TC), jnp.bfloat16),
            pltpu.VMEM((2, 2 * ROWS, 2 * ROWS), jnp.float32),
            pltpu.VMEM((2, 2, 2, ROWS, ROWS), jnp.bfloat16),
            dma((2 * NC,)), dma((2 * NC,)), dma((2 * NC,)), dma((2 * NC,)),
            dma((NC,)), dma((NC,)), dma((NC,)), dma((NC,)), dma((NC,)), dma((NC,)), dma((NC,)), dma((NC,)),
            dma((NC,)), dma((NC,)), dma((2, 2)),
        ],
        compiler_params=pltpu.CompilerParams(
            collective_id=0, has_side_effects=True, vmem_limit_bytes=46 * 1024 * 1024
        ),
        cost_estimate=pl.CostEstimate(flops=26 * 10**9, bytes_accessed=6 * 2**20, transcendentals=0),
        name="correlate",
    )(samples, rfi_flags, feed_map.reshape(16, 128))


def solution(mesh):
    in_specs = (P(("freq", "pair"), None, None, None), P("freq", None), P())
    out_specs = P("freq", None, "pair", None)
    return jax.shard_map(local, mesh=mesh, in_specs=in_specs, out_specs=out_specs, check_vma=False)
```

```python
import jax
import jax.numpy as jnp
from jax import lax
from jax.experimental import pallas as pl
from jax.experimental.pallas import tpu as pltpu
from jax.sharding import PartitionSpec as P

MESH = pl.DeviceIdType.MESH
NC = 8
TC = 128
SLOTS = 2048
ROWS = 512


def kernel(raw, table, out, samples, zbuf, obuf, g, onehot, merged, ordered, left, acc, staged,
           zs, zr, xs, xr, own_s, own_r, out_s, out_r, fwd_s, fwd_r, core_s, core_r, pair_s, pair_r, write_s):
    fi = lax.axis_index("freq")
    member = lax.axis_index("pair")
    yh, z, x = fi // 32, (fi // 4) % 8, fi % 4
    yl, core = member // 2, member % 2
    y = yh * 2 + yl
    y_inner = yh * 2 + 1 - yl
    y_outer = 3 - y
    y_far = (1 - yh) * 2 + yl
    zpeers = [lax.rem(z + d, 8) for d in (4, 3, 5, 2, 6, 1, 7)]
    xpeers = [lax.rem(x + d, 4) for d in (2, 1, 3)]

    def device(yy, zz, xx, cc):
        return ((yy // 2 * 8 + zz) * 4 + xx, yy % 2 * 2 + cc)

    inner = device(y_inner, z, x, core)
    outer = device(y_outer, z, x, core)
    sibling = device(y, z, x, 1 - core)

    def remote(src, dst, send, recv, target):
        return pltpu.make_async_remote_copy(
            src_ref=src, dst_ref=dst, send_sem=send, recv_sem=recv, device_id=target, device_id_type=MESH
        )

    def wait(ref, sem):
        pltpu.make_async_copy(ref, ref, sem).wait()

    barrier = pltpu.get_barrier_semaphore()
    targets = [device(y, zz, x, core) for zz in zpeers] + [device(y, z, xx, core) for xx in xpeers]
    targets += [inner, outer, sibling]
    for target in targets:
        pl.semaphore_signal(barrier, inc=1, device_id=target, device_id_type=MESH)

    def pack(k):
        times = pl.ds(pl.multiple_of(k * TC, TC), TC)

        @pl.loop(0, 8)
        def _(b):
            block = raw[:, pl.ds(pl.multiple_of(b * 8, 8), 8), :, times]
            packed = jnp.transpose(block, (1, 2, 0, 3)).reshape(2, 4, 16, TC)
            samples[k, b // 4, pl.ds(pl.multiple_of(b % 4 * 2, 2), 2)] = packed


    def z_send(j):
        k, h = j // 2, j % 2
        half = jnp.where(h == 0, 1 - yh, yh)
        pltpu.make_async_copy(samples.at[k, half, z], zbuf.at[j, z], zr.at[j]).start()
        for zz in zpeers:
            remote(samples.at[k, half, zz], zbuf.at[j, z], zs.at[j], zr.at[j], device(y, zz, x, core)).start()

    def x_send(k, h):
        j = 2 * k + h
        wait(zbuf.at[j], zr.at[j])
        dst = g.at[k, core, y, x] if h else obuf.at[k, x]
        pltpu.make_async_copy(zbuf.at[j, :, x], dst, xr.at[j]).start()
        for xx in xpeers:
            remote(zbuf.at[j, :, xx], dst, xs.at[j], xr.at[j], device(y, z, xx, core)).start()

    def core_send(k, yy):
        remote(g.at[k, core, yy], g.at[k, core, yy], core_s.at[k], core_r.at[k], sibling).start()

    def y_send(k, h):
        j = 2 * k + h
        if h:
            wait(g.at[k, core, y], xr.at[j])
            remote(g.at[k, core, y], g.at[k, core, y], own_s.at[k], own_r.at[k], inner).start()
            core_send(k, y)
        else:
            wait(obuf.at[k], xr.at[j])
            remote(obuf.at[k], g.at[k, core, y], out_s.at[k], out_r.at[k], outer).start()

    def forward(k):
        block = g.at[k, core, y_outer]
        wait(block, out_r.at[k])
        remote(block, block, fwd_s.at[k], fwd_r.at[k], inner).start()
        core_send(k, y_outer)

    def own_arrived(k):
        wait(g.at[k, core, y_inner], own_r.at[k])
        core_send(k, y_inner)

    def forward_arrived(k):
        wait(g.at[k, core, y_far], fwd_r.at[k])
        core_send(k, y_far)

    def order(k):
        wait(g.at[k, 1 - core], core_r.at[k])
        keep = jnp.broadcast_to((1 - table[pl.ds(k, 1), :]).astype(jnp.float32), (16, TC)).astype(jnp.bfloat16)

        @pl.loop(0, 8)
        def _(b):
            rows = pl.ds(pl.multiple_of(b * 256, 256), 256)
            block = g[k, b // 4, b % 4].reshape(32, 16, TC) * keep
            merged[rows, :TC] = block[:, :8].reshape(256, TC)
            merged[rows, TC:] = block[:, 8:].reshape(256, TC)

        picked = jnp.dot(onehot[...], merged[...], preferred_element_type=jnp.float32).astype(jnp.bfloat16)
        ordered[k, :, core] = picked.reshape(2, ROWS, 2 * TC)
        pair_copy(k).start()

    def pair_copy(k):
        block = ordered.at[k, :, core]
        return remote(block, block, pair_s.at[k], pair_r.at[k], sibling)

    def prepare_left(k):
        own = ordered[k, yl, core]
        left[:ROWS, :] = own
        left[ROWS:, :TC] = own[:, TC:]
        left[ROWS:, TC:] = -own[:, :TC]

    def multiply(k, half):
        return lax.dot_general(
            left[...],
            ordered[k, :, half].reshape(2 * ROWS, 2 * TC),
            (((1,), (1,)), ((), ())),
            preferred_element_type=jnp.float32,
        )

    def write(half, i):
        columns = pl.ds(pl.multiple_of((i * 2 + half) * ROWS, ROWS), ROWS)
        return pltpu.make_async_copy(staged.at[half, i], out.at[0, :, :, columns], write_s.at[half, i])

    def product(k, half):
        @pl.when(k < NC - 1)
        def _():
            acc[half] += multiply(k, half)

        @pl.when(k == NC - 1)
        def _():
            total = (acc[half] + multiply(k, half)) * (1.0 / (NC * TC))
            for i in range(2):
                staged[half, i] = total[:, i * ROWS : (i + 1) * ROWS].astype(jnp.bfloat16).reshape(2, ROWS, ROWS)
                write(half, i).start()

    pack(0)
    pl.semaphore_wait(barrier, len(targets))
    z_send(0)
    z_send(1)
    pack(1)
    z_send(2)
    z_send(3)

    @pl.loop(0, 8)
    def _(b):
        feed = table[pl.ds(NC + (b // 4 * 2 + core) * 4 + b % 4, 1), :]
        w, c, l = feed & 7, (feed >> 3) & 1, (feed >> 4) & 1
        xx, zz, h = (feed >> 5) & 3, (feed >> 7) & 7, feed >> 10
        spot = ((((c * 4 + h * 2 + l) * 4 + xx) * 8 + zz) * 8 + w).astype(jnp.float32)
        spot = jnp.broadcast_to(spot, (128, 128)).T.astype(jnp.int32)
        for n in range(SLOTS // 128):
            hit = spot == lax.broadcasted_iota(jnp.int32, (128, 128), 1) + n * 128
            onehot[pl.ds(pl.multiple_of(b * 128, 128), 128), n * 128 : (n + 1) * 128] = jnp.where(
                hit, 1.0, 0.0
            ).astype(jnp.bfloat16)

    for half in range(2):
        acc[half] = jnp.zeros((2 * ROWS, 2 * ROWS), jnp.float32)

    def step(s, carry):
        @pl.when(s < NC)
        def _():
            x_send(s, 0)

        @pl.when(s + 2 < NC)
        def _():
            pack(s + 2)
            z_send(2 * s + 4)

        @pl.when((s >= 1) & (s < NC + 1))
        def _():
            y_send((s - 1), 0)

        @pl.when((s >= 3) & (s < NC + 3))
        def _():
            forward_arrived((s - 3))

        @pl.when(s < NC)
        def _():
            x_send(s, 1)

        @pl.when(s + 2 < NC)
        def _():
            z_send(2 * s + 5)

        @pl.when((s >= 1) & (s < NC + 1))
        def _():
            y_send((s - 1), 1)

        @pl.when(s >= 4)
        def _():
            order((s - 4))

        @pl.when(s >= 4)
        def _():
            prepare_left((s - 4))
            product((s - 4), core)

        @pl.when((s >= 2) & (s < NC + 2))
        def _():
            own_arrived((s - 2))

        @pl.when(s >= 4)
        def _():
            wait(ordered.at[(s - 4), :, 1 - core], pair_r.at[(s - 4)])
            product((s - 4), 1 - core)

        @pl.when((s >= 1) & (s < NC + 1))
        def _():
            forward((s - 1))

        return carry

    lax.fori_loop(0, NC + 4, step, 0)

    @pl.loop(0, NC)
    def _(k):
        for h in range(2):
            wait(zbuf.at[2 * k + h, pl.ds(0, 7)], zs.at[2 * k + h])
            wait(obuf.at[k, pl.ds(0, 3)], xs.at[2 * k + h])
        wait(obuf.at[k], own_s.at[k])
        wait(obuf.at[k], out_s.at[k])
        wait(obuf.at[k], fwd_s.at[k])
        wait(g.at[k, 0], core_s.at[k])
        wait(ordered.at[k, :, core], pair_s.at[k])

    for half in range(2):
        for i in range(2):
            write(half, i).wait()


def local(samples, rfi_flags, feed_map):
    dma = pltpu.SemaphoreType.DMA
    vmem = pl.BlockSpec(memory_space=pltpu.VMEM)
    return pl.pallas_call(
        kernel,
        out_shape=jax.ShapeDtypeStruct((1, 2, ROWS, SLOTS), jnp.bfloat16),
        in_specs=[vmem, vmem],
        out_specs=pl.BlockSpec(memory_space=pl.ANY),
        scratch_shapes=[
            pltpu.VMEM((NC, 2, 8, 4, 16, TC), jnp.bfloat16),
            pltpu.VMEM((2 * NC, 8, 4, 16, TC), jnp.bfloat16),
            pltpu.VMEM((NC, 4, 8, 16, TC), jnp.bfloat16),
            pltpu.VMEM((NC, 2, 4, 4, 8, 16, TC), jnp.bfloat16),
            pltpu.VMEM((2 * ROWS, SLOTS), jnp.bfloat16),
            pltpu.VMEM((SLOTS, 2 * TC), jnp.bfloat16),
            pltpu.VMEM((NC, 2, 2, ROWS, 2 * TC), jnp.bfloat16),
            pltpu.VMEM((2 * ROWS, 2 * TC), jnp.bfloat16),
            pltpu.VMEM((2, 2 * ROWS, 2 * ROWS), jnp.float32),
            pltpu.VMEM((2, 2, 2, ROWS, ROWS), jnp.bfloat16),
            dma((2 * NC,)), dma((2 * NC,)), dma((2 * NC,)), dma((2 * NC,)),
            dma((NC,)), dma((NC,)), dma((NC,)), dma((NC,)), dma((NC,)), dma((NC,)), dma((NC,)), dma((NC,)),
            dma((NC,)), dma((NC,)), dma((2, 2)),
        ],
        compiler_params=pltpu.CompilerParams(
            collective_id=0, has_side_effects=True, vmem_limit_bytes=46 * 1024 * 1024
        ),
        cost_estimate=pl.CostEstimate(flops=26 * 10**9, bytes_accessed=6 * 2**20, transcendentals=0),
        name="correlate",
    )(samples, jnp.concatenate([rfi_flags.reshape(NC, TC), feed_map.reshape(16, TC)]))


def solution(mesh):
    in_specs = (P(("freq", "pair"), None, None, None), P("freq", None), P())
    out_specs = P("freq", None, "pair", None)
    return jax.shard_map(local, mesh=mesh, in_specs=in_specs, out_specs=out_specs, check_vma=False)
```
